256 devices in a mesh: rcv: 32 (over x, z), src: 8 (over y, core).
Axes of the slice: x: 4, y: 4, z: 8, core: 2. Of those that a mesh axis runs over, the one named last changes fastest.
Arguments:
- reflectivity: bfloat16 [2, 1, 2048, 2048], P(None, None, 'rcv', 'src'), may hold values from -0.09375 to 0.09375
- downgoing: bfloat16 [2, 1, 2048, 4096], P(None, None, 'rcv', 'src'), may hold values from -6 to 6
- upgoing: bfloat16 [2, 1, 2048, 4096], P(None, None, 'rcv', 'src'), may hold values from -6 to 6
- recorded: int32 [256, 20], P('rcv'), may hold values from 0 to 31, as said below
Outputs:
- residual: float32 [2, 1, 2048, 4096], P(None, None, 'rcv', 'src')
- grad_reflect: float32 [2, 1, 2048, 2048], P(None, None, 'rcv', 'src')
- grad_downgoing: float32 [2, 1, 2048, 4096], P(None, None, 'rcv', 'src')
The draws below stay inside these ranges and needn't reach their ends.
Inputs may be any that keep to these rules, and one draw needn't show every extreme that they name: `recorded`: each row lists 20 distinct source blocks.
All inputs are finite; a program needn't handle non-finite values.
Results may differ from the reference program's by a relative error of at most 0.0003.
Values may be sent and summed in bfloat16 or wider, within the bound.
No kernel may reach another device: no remote copies, remote signals or barrier semaphores. Data moves between devices by JAX's collectives and lax.ppermute only.
A program may use at most 64 MiB of HBM per device.

```python
import jax
import jax.numpy as jnp
from jax import lax

FREQ = 1
VIRT = 2048
RBLK = 8
SBLK = 128
NR = 2048
NS = 4096
NRB = 256
NSB = 32
KREC = 20


def draw_recorded(key, part):
    key = jax.random.fold_in(key, 7)
    scores = jax.random.randint(key, (NRB, NSB), 0, 1 << 20) * NSB + jnp.arange(NSB, dtype=jnp.int32)[None, :]
    rows = jnp.arange(NRB, dtype=jnp.int32)[:, None]
    cols = jnp.arange(NSB, dtype=jnp.int32)[None, :]
    scores = jnp.where((rows == 0) & (cols == NSB - 1), -1, scores)
    scores = jnp.where((rows == 1) & (cols == 0), -1, scores)
    order = jnp.argsort(scores, axis=1)
    return order[:, :KREC].astype(jnp.int32)


def steps_of(stream_key, extent, shards, low, largest):
    def one(position, parts):
        steps = jax.random.uniform(jax.random.fold_in(jax.random.fold_in(stream_key, 6), position), (parts,), jnp.float32, low / len(shards), largest / len(shards))
        return jnp.repeat(jnp.exp(steps), extent[position] // parts).reshape((-1,) + (1,) * (len(extent) - position - 1))

    loudness = one(*shards[0])
    for cut in shards[1:]:
        loudness = loudness * one(*cut)
    return loudness


def gaussian(own_key, extent, deviation, most, shards=(), kind=jnp.bfloat16):
    values = jax.random.normal(own_key, extent, jnp.float32) * deviation
    if len(shards) > 0:
        values = steps_of(own_key, extent, shards, -0.22, 0.18) * values
    return jnp.clip(values, min=-most, max=most).astype(kind)


def setup_inputs(seed: int = 0) -> dict:
    key_of = jax.random.split(jax.random.key(seed), 5)
    reflectivity = gaussian(key_of[0], (2, FREQ, NR, VIRT), (2 * VIRT) ** -0.5, 0.09375, ((2, 32), (3, 8)))
    downgoing = gaussian(key_of[1], (2, FREQ, VIRT, NS), 1.0, 6.0, ((2, 32), (3, 8)))
    upgoing = gaussian(key_of[2], (2, FREQ, NR, NS), 1.0, 6.0, ((2, 32), (3, 8)))
    recorded = draw_recorded(jax.random.fold_in(key_of[4], 71), 0)
    return {"reflectivity": reflectivity, "downgoing": downgoing, "upgoing": upgoing, "recorded": recorded}


def complex_product(left_real, left_imag, right_real, right_imag, form):
    real_out = jnp.einsum(form, left_real, right_real) - jnp.einsum(form, left_imag, right_imag)
    imag_out = jnp.einsum(form, left_real, right_imag) + jnp.einsum(form, left_imag, right_real)
    return real_out, imag_out


def highest(form, left, right):
    return jnp.einsum(form, left, right, precision=lax.Precision.HIGHEST)


def reference(reflectivity, downgoing, upgoing, recorded):
    block_ids = jnp.arange(NSB, dtype=jnp.int32)
    block_hits = jnp.any(recorded[:, :, None] == block_ids[None, None, :], axis=1).astype(jnp.float32)
    record_mask = jnp.repeat(jnp.repeat(block_hits, RBLK, axis=0), SBLK, axis=1)
    refl = reflectivity.astype(jnp.float32)
    wave = downgoing.astype(jnp.float32)
    pred_real, pred_imag = complex_product(refl[0], refl[1], wave[0], wave[1], "frv,fvs->frs")
    upper = upgoing.astype(jnp.float32)
    resid = jnp.stack([record_mask * (pred_real - upper[0]), record_mask * (pred_imag - upper[1])])
    grad_r_real = highest("frs,fvs->frv", resid[0], wave[0]) + highest("frs,fvs->frv", resid[1], wave[1])
    grad_r_imag = highest("frs,fvs->frv", resid[1], wave[0]) - highest("frs,fvs->frv", resid[0], wave[1])
    grad_reflect = jnp.stack([grad_r_real, grad_r_imag]) * (NS ** -0.5)
    grad_w_real = highest("frv,frs->fvs", refl[0], resid[0]) + highest("frv,frs->fvs", refl[1], resid[1])
    grad_w_imag = highest("frv,frs->fvs", refl[0], resid[1]) - highest("frv,frs->fvs", refl[1], resid[0])
    grad_downgoing = jnp.stack([grad_w_real, grad_w_imag]) * (NR ** -0.5)
    return resid, grad_reflect, grad_downgoing
```

```python
import jax
import jax.numpy as jnp
from jax import lax
from jax.experimental import pallas as pl
from jax.experimental.pallas import tpu as pltpu
from jax.sharding import Mesh, PartitionSpec as P

RBLK = 8
SBLK = 128
X, Z, Y, C = 4, 8, 4, 2
BF, F32 = jnp.bfloat16, jnp.float32
VMEM = pl.BlockSpec(memory_space=pltpu.VMEM)
SMEM = pl.BlockSpec(memory_space=pltpu.SMEM)
PARAMS = pltpu.CompilerParams(vmem_limit_bytes=40 * 1024 * 1024)


def send(value, axis, size, step):
    return lax.ppermute(value, axis, [(i, (i + step) % size) for i in range(size)])


def pack_kernel(place, wave, up, recorded, packed):
    rec = recorded[...]
    for k in range(X):
        lanes = slice(k * SBLK, (k + 1) * SBLK)
        packed[k, 0:64, :] = wave[0, :, lanes]
        packed[k, 64:128, :] = wave[1, :, lanes]
        packed[k, 128:192, :] = up[0, :, lanes]
        packed[k, 192:256, :] = up[1, :, lanes]
        block = place[3] + k
        hit = jnp.max(jnp.where(rec == block, 1.0, 0.0), axis=1, keepdims=True)
        rows = jnp.broadcast_to(hit, (8, SBLK))
        packed[k, 256:272, :] = jnp.concatenate([rows, rows], axis=0).astype(BF)


def wave_block(wave, y_src, half):
    parts = [wave[4 * half + q, y_src] for q in range(4)]
    real = jnp.concatenate([p[0:64] for p in parts], axis=0)
    imag = jnp.concatenate([p[64:128] for p in parts], axis=0)
    return jnp.concatenate([real, imag], axis=1)


def refl_block(refl, yr):
    return jnp.concatenate([r[yr].reshape(128, 256) for r in refl], axis=0)


def residual_kernel(place, o0, o1, o2, o3, s0, s1, s2, s3, wave, packed, res, own, other, high, low):
    mx, my, mc = place[0], place[1], place[2]
    mine, theirs = (o0, o1, o2, o3), (s0, s1, s2, s3)
    acc = jnp.zeros((512, 256), F32)
    for yr in range(Y):
        y_src = lax.rem(my - yr + Y, Y)
        for refl, half in ((mine, mc), (theirs, 1 - mc)):
            acc += jnp.dot(
                refl_block(refl, yr), wave_block(wave, y_src, half), preferred_element_type=F32
            )
    for xr in range(X):
        x_src = lax.rem(mx - xr + X, X)
        a = acc[xr * 128 : xr * 128 + 64]
        b = acc[xr * 128 + 64 : xr * 128 + 128]
        hits = packed[x_src, 256:272, :].astype(F32)
        mask = jnp.concatenate(
            [jnp.broadcast_to(hits[r : r + 1], (RBLK, SBLK)) for r in range(8)], axis=0
        )
        real = mask * (a[:, :128] - b[:, 128:] - packed[x_src, 128:192, :].astype(F32))
        imag = mask * (a[:, 128:] + b[:, :128] - packed[x_src, 192:256, :].astype(F32))
        res[xr, 0] = real
        res[xr, 1] = imag
        top, bottom = slice(xr * 128, xr * 128 + 64), slice(xr * 128 + 64, xr * 128 + 128)
        rh, ih = real.astype(BF), imag.astype(BF)
        rl, il = (real - rh.astype(F32)).astype(BF), (imag - ih.astype(F32)).astype(BF)
        for out, re, im in ((high, rh, ih), (low, rl, il)):
            out[top, 0:128] = re
            out[top, 128:256] = im
            out[bottom, 0:128] = im
            out[bottom, 128:256] = -re
    for yr in range(Y):
        y_src = lax.rem(my - yr + Y, Y)
        for out, half in ((other, 1 - mc), (own, mc)):
            w = wave_block(wave, y_src, half)
            dims = (((1,), (1,)), ((), ()))
            g = lax.dot_general(high[...], w, dims, preferred_element_type=F32)
            g += lax.dot_general(low[...], w, dims, preferred_element_type=F32)
            out[yr] = g.reshape(X, 2, 64, 256)


def wave_grad_kernel(place, o0, o1, o2, o3, s0, s1, s2, s3, high, low, out):
    my, mc = place[1], place[2]
    mine, theirs = (o0, o1, o2, o3), (s0, s1, s2, s3)
    for yr in range(Y):
        y_src = lax.rem(my - yr + Y, Y)
        for refl, half in ((mine, mc), (theirs, 1 - mc)):
            r = refl_block(refl, yr)
            dims = (((0,), (0,)), ((), ()))
            g = lax.dot_general(r, high[...], dims, preferred_element_type=F32)
            g += lax.dot_general(r, low[...], dims, preferred_element_type=F32)
            for q in range(4):
                to = y_src * Z + 4 * half + q
                out[to, 0] = g[q * 64 : q * 64 + 64, 0:128]
                out[to, 1] = g[q * 64 : q * 64 + 64, 128:256]


def finish_kernel(scale, place, parts, r0, r1, r2, r3, wave_out, res_out):
    mx = place[0]
    for k in range(X):
        lanes = slice(k * SBLK, (k + 1) * SBLK)
        for p in range(2):
            total = parts[k * Z, p]
            for z in range(1, Z):
                total = total + parts[k * Z + z, p]
            wave_out[p, :, lanes] = total * scale
    for k, piece in enumerate((r0, r1, r2, r3)):
        at = pl.multiple_of(lax.rem(mx + k, X) * SBLK, SBLK)
        for p in range(2):
            res_out[p, :, pl.ds(at, SBLK)] = piece[p]


def kernel_call(body, outs, n_in, name):
    return pl.pallas_call(
        body,
        out_shape=[jax.ShapeDtypeStruct(s, d) for s, d in outs],
        in_specs=[SMEM] + [VMEM] * n_in,
        out_specs=[VMEM] * len(outs),
        compiler_params=PARAMS,
        name=name,
    )


def shards(reflectivity, downgoing, upgoing, recorded):
    mx, my, mc = lax.axis_index("x"), lax.axis_index("y"), lax.axis_index("c")
    place = jnp.stack([mx, my, mc, (my * C + mc) * X]).astype(jnp.int32)
    refl = reflectivity[:, 0]

    gathered = jnp.stack([refl] + [send(refl, "y", Y, k) for k in range(1, Y)])
    mine = [gathered] + [send(gathered, "x", X, k) for k in range(1, X)]
    theirs = [send(m, "c", C, 1) for m in mine]

    (packed,) = kernel_call(pack_kernel, [((X, 272, 128), BF)], 3, "pack")(
        place, downgoing[:, 0], upgoing[:, 0], recorded
    )
    packed = lax.all_to_all(packed, "x", split_axis=0, concat_axis=0, tiled=True)
    wave = lax.all_gather(packed[:, :128], "z", axis=0)

    res, own, other, high, low = kernel_call(
        residual_kernel,
        [
            ((X, 2, 64, 128), F32),
            ((Y, X, 2, 64, 256), F32),
            ((Y, X, 2, 64, 256), F32),
            ((512, 256), BF),
            ((512, 256), BF),
        ],
        10,
        "residual",
    )(place, *mine, *theirs, wave, packed)
    other = send(other, "c", C, 1)
    (wave_part,) = kernel_call(wave_grad_kernel, [((X * Z, 2, 64, 128), F32)], 10, "wave_grad")(
        place, *mine, *theirs, high, low
    )
    pieces = [res[0]] + [send(res[k], "x", X, -k) for k in range(1, X)]
    sums = own[0] + other[0]
    for k in range(1, Y):
        sums = sums + send(own[k] + other[k], "y", Y, -k)
    grad = sums[0]
    for k in range(1, X):
        grad = grad + send(sums[k], "x", X, -k)
    n_rec, n_src = Z * X * 64, Y * C * 512
    grad_reflect = (grad * n_src ** (-0.5))[:, None]

    wave_part = lax.all_to_all(wave_part, ("x", "z"), split_axis=0, concat_axis=0, tiled=True)

    def finish(*refs):
        finish_kernel(n_rec ** (-0.5), *refs)

    grad_downgoing, residual = kernel_call(
        finish, [((2, 64, 512), F32), ((2, 64, 512), F32)], 5, "finish"
    )(place, wave_part, *pieces)
    return residual[:, None], grad_reflect, grad_downgoing[:, None]


def solution(mesh):
    fine = Mesh(mesh.devices.reshape(X, Z, Y, C), ("x", "z", "y", "c"))
    spec = P(None, None, ("x", "z"), ("y", "c"))
    return jax.shard_map(
        shards,
        mesh=fine,
        in_specs=(spec, spec, spec, P(("x", "z"), None)),
        out_specs=(spec, spec, spec),
        check_vma=False,
    )
```

```python
import jax
import jax.numpy as jnp
from jax import lax
from jax.experimental import pallas as pl
from jax.experimental.pallas import tpu as pltpu
from jax.sharding import Mesh, PartitionSpec as P

RBLK = 8
SBLK = 128
X, Z, Y, C = 4, 8, 4, 2
BF, F32 = jnp.bfloat16, jnp.float32
VMEM = pl.BlockSpec(memory_space=pltpu.VMEM)
HBM = pl.BlockSpec(memory_space=pltpu.HBM)
ANY = pl.BlockSpec(memory_space=pl.ANY)
SMEM = pl.BlockSpec(memory_space=pltpu.SMEM)
PARAMS = pltpu.CompilerParams(vmem_limit_bytes=16 * 1024 * 1024)


def send(value, axis, size, step):
    return lax.ppermute(value, axis, [(i, (i + step) % size) for i in range(size)])


def pack_kernel(place, wave_in, up_in, rec_in, packed, m0, m1, m2, m3, wave, up, rec, sems):
    copies = [
        pltpu.make_async_copy(src, dst, sems.at[i])
        for i, (src, dst) in enumerate(((wave_in, wave), (up_in, up), (rec_in, rec)))
    ]
    for copy in copies:
        copy.start()
    for copy in copies:
        copy.wait()
    for k in range(X):
        lanes = slice(k * SBLK, (k + 1) * SBLK)
        for p in range(2):
            part = wave[p, :, lanes]
            for z in range(Z):
                packed[k * Z + z, p * 64 : p * 64 + 64, :] = part
    recs = rec[...]
    for k, out in enumerate((m0, m1, m2, m3)):
        to = lax.rem(place[0] + k, X)
        at = pl.multiple_of(to * SBLK, SBLK)
        out[0:64, :] = up[0, :, pl.ds(at, SBLK)]
        out[64:128, :] = up[1, :, pl.ds(at, SBLK)]
        hit = jnp.max(jnp.where(recs == place[3] + to, 1.0, 0.0), axis=1, keepdims=True)
        rows = jnp.broadcast_to(hit, (8, SBLK))
        out[128:144, :] = jnp.concatenate([rows, rows], axis=0).astype(BF)


def wave_block(wave, y_src, half):
    parts = [wave[y_src * Z + 4 * half + q] for q in range(4)]
    real = jnp.concatenate([p[0:64] for p in parts], axis=0)
    imag = jnp.concatenate([p[64:128] for p in parts], axis=0)
    return jnp.concatenate([real, imag], axis=1)


def refl_block(refl, yr):
    return jnp.concatenate([r[yr].reshape(128, 256) for r in refl], axis=0)


def residual_kernel(place, o0, o1, o2, o3, s0, s1, s2, s3, wave, m0, m1, m2, m3, res0, res1, res2, res3, other, high, low):
    my, mc = place[1], place[2]
    mine, theirs = (o0, o1, o2, o3), (s0, s1, s2, s3)
    acc = jnp.zeros((512, 256), F32)
    for yr in range(Y):
        y_src = lax.rem(my - yr + Y, Y)
        for refl, half in ((mine, mc), (theirs, 1 - mc)):
            acc += jnp.dot(
                refl_block(refl, yr), wave_block(wave, y_src, half), preferred_element_type=F32
            )
    for xr, (data, res) in enumerate(zip((m0, m1, m2, m3), (res0, res1, res2, res3))):
        a = acc[xr * 128 : xr * 128 + 64]
        b = acc[xr * 128 + 64 : xr * 128 + 128]
        hits = data[128:144, :].astype(F32)
        mask = jnp.concatenate(
            [jnp.broadcast_to(hits[r : r + 1], (RBLK, SBLK)) for r in range(8)], axis=0
        )
        real = mask * (a[:, :128] - b[:, 128:] - data[0:64, :].astype(F32))
        imag = mask * (a[:, 128:] + b[:, :128] - data[64:128, :].astype(F32))
        res[0] = real
        res[1] = imag
        top, bottom = slice(xr * 128, xr * 128 + 64), slice(xr * 128 + 64, xr * 128 + 128)
        rh, ih = real.astype(BF), imag.astype(BF)
        rl, il = (real - rh.astype(F32)).astype(BF), (imag - ih.astype(F32)).astype(BF)
        for out, re, im in ((high, rh, ih), (low, rl, il)):
            out[top, 0:128] = re
            out[top, 128:256] = im
            out[bottom, 0:128] = im
            out[bottom, 128:256] = -re
    refl_grad(my, 1 - mc, wave, high, low, other)


def refl_grad(my, half, wave, high, low, out):
    for yr in range(Y):
        w = wave_block(wave, lax.rem(my - yr + Y, Y), half)
        dims = (((1,), (1,)), ((), ()))
        g = lax.dot_general(high[...], w, dims, preferred_element_type=F32)
        g += lax.dot_general(low[...], w, dims, preferred_element_type=F32)
        out[yr] = g.reshape(X, 2, 64, 256)


def grads_kernel(place, o0, o1, o2, o3, s0, s1, s2, s3, wave, high, low, out, own):
    my, mc = place[1], place[2]
    mine, theirs = (o0, o1, o2, o3), (s0, s1, s2, s3)
    for yr in range(Y):
        y_src = lax.rem(my - yr + Y, Y)
        for refl, half in ((mine, mc), (theirs, 1 - mc)):
            r = refl_block(refl, yr)
            dims = (((0,), (0,)), ((), ()))
            g = lax.dot_general(r, high[...], dims, preferred_element_type=F32)
            g += lax.dot_general(r, low[...], dims, preferred_element_type=F32)
            for q in range(4):
                to = y_src * Z + 4 * half + q
                out[to, 0] = g[q * 64 : q * 64 + 64, 0:128]
                out[to, 1] = g[q * 64 : q * 64 + 64, 128:256]
    refl_grad(my, mc, wave, high, low, own)


def sum_kernel(place, own, other, wave_part, s0, s1, s2, s3, wave_out):
    for k, out in enumerate((s0, s1, s2, s3)):
        out[...] = own[k] + other[k]


def finish_kernel(scale, place, parts, r0, r1, r2, r3, wave_out, res_out):
    mx = place[0]
    for k in range(X):
        lanes = slice(k * SBLK, (k + 1) * SBLK)
        for p in range(2):
            total = parts[k * Z, p]
            for z in range(1, Z):
                total = total + parts[k * Z + z, p]
            wave_out[p, :, lanes] = total * scale
    for k, piece in enumerate((r0, r1, r2, r3)):
        at = pl.multiple_of(lax.rem(mx + k, X) * SBLK, SBLK)
        for p in range(2):
            res_out[p, :, pl.ds(at, SBLK)] = piece[p]


def kernel_call(body, outs, ins, name, out_specs=None, scratch=(), aliases={}):
    return pl.pallas_call(
        body,
        out_shape=[jax.ShapeDtypeStruct(s, d) for s, d in outs],
        in_specs=[SMEM] + ins,
        out_specs=out_specs or [VMEM] * len(outs),
        scratch_shapes=scratch,
        input_output_aliases=aliases,
        compiler_params=PARAMS,
        name=name,
    )


def shards(reflectivity, downgoing, upgoing, recorded):
    mx, my, mc = lax.axis_index("x"), lax.axis_index("y"), lax.axis_index("c")
    place = jnp.stack([mx, my, mc, (my * C + mc) * X]).astype(jnp.int32)
    refl = reflectivity[:, 0]

    gathered = jnp.stack([refl] + [send(refl, "y", Y, k) for k in range(1, Y)])
    mine = [gathered] + [send(gathered, "x", X, k) for k in range(1, X)]
    theirs = [send(m, "c", C, 1) for m in mine]

    wave, *data = kernel_call(
        pack_kernel,
        [((X * Z, 128, 128), BF)] + [((144, 128), BF)] * X,
        [HBM] * 3,
        "pack",
        scratch=[
            pltpu.VMEM((2, 64, 512), BF),
            pltpu.VMEM((2, 64, 512), BF),
            pltpu.VMEM((8, 20), jnp.int32),
            pltpu.SemaphoreType.DMA((3,)),
        ],
    )(place, downgoing[:, 0], upgoing[:, 0], recorded)
    wave = lax.all_to_all(wave, ("x", "z"), split_axis=0, concat_axis=0, tiled=True)
    data = [data[0]] + [send(data[k], "x", X, k) for k in range(1, X)]

    *pieces, other, high, low = kernel_call(
        residual_kernel,
        [((2, 64, 128), F32)] * X + [((Y, X, 2, 64, 256), F32)] + [((512, 256), BF)] * 2,
        [VMEM] * 13,
        "residual",
    )(place, *mine, *theirs, wave, *data)
    other = send(other, "c", C, 1)
    wave_part, own = kernel_call(
        grads_kernel,
        [((X * Z, 2, 64, 128), F32), ((Y, X, 2, 64, 256), F32)],
        [VMEM] * 11,
        "grads",
    )(place, *mine, *theirs, wave, high, low)
    *sums, wave_part = kernel_call(
        sum_kernel,
        [((X, 2, 64, 256), F32)] * Y + [((X * Z, 2, 64, 128), F32)],
        [VMEM, VMEM, ANY],
        "sums",
        out_specs=[VMEM] * Y + [ANY],
        aliases={3: Y},
    )(place, own, other, wave_part)
    pieces = [pieces[0]] + [send(pieces[k], "x", X, -k) for k in range(1, X)]
    total = sums[0]
    for k in range(1, Y):
        total = total + send(sums[k], "y", Y, -k)
    grad = total[0]
    for k in range(1, X):
        grad = grad + send(total[k], "x", X, -k)
    n_rec, n_src = Z * X * 64, Y * C * 512
    grad_reflect = (grad * n_src ** (-0.5))[:, None]

    wave_part = lax.all_to_all(wave_part, ("x", "z"), split_axis=0, concat_axis=0, tiled=True)

    def finish(*refs):
        finish_kernel(n_rec ** (-0.5), *refs)

    grad_downgoing, residual = kernel_call(
        finish, [((2, 64, 512), F32), ((2, 64, 512), F32)], [VMEM] * 5, "finish"
    )(place, wave_part, *pieces)
    return residual[:, None], grad_reflect, grad_downgoing[:, None]


def solution(mesh):
    fine = Mesh(mesh.devices.reshape(X, Z, Y, C), ("x", "z", "y", "c"))
    spec = P(None, None, ("x", "z"), ("y", "c"))
    return jax.shard_map(
        shards,
        mesh=fine,
        in_specs=(spec, spec, spec, P(("x", "z"), None)),
        out_specs=(spec, spec, spec),
        check_vma=False,
    )
```

```python
import jax
import jax.numpy as jnp
from jax import lax
from jax.experimental import pallas as pl
from jax.experimental.pallas import tpu as pltpu
from jax.sharding import Mesh, PartitionSpec as P

RBLK = 8
SBLK = 128
X, Z, Y, C = 4, 8, 4, 2
BF, F32, I16 = jnp.bfloat16, jnp.float32, jnp.int16
VMEM = pl.BlockSpec(memory_space=pltpu.VMEM)
ANY = pl.BlockSpec(memory_space=pl.ANY)
SMEM = pl.BlockSpec(memory_space=pltpu.SMEM)
PARAMS = pltpu.CompilerParams(vmem_limit_bytes=16 * 1024 * 1024)


def send(value, axis, size, step):
    return lax.ppermute(value, axis, [(i, (i + step) % size) for i in range(size)])


def pack_kernel(place, r0, r1, r2, r3, wave, up, rec, packed, m0, m1, m2, m3):
    for k in range(X):
        lanes = slice(k * SBLK, (k + 1) * SBLK)
        for p in range(2):
            part = wave[p, :, lanes]
            for z in range(Z):
                packed[k * Z + z, p * 64 : p * 64 + 64, :] = part
    recs = rec[...]
    for k, out in enumerate((m0, m1, m2, m3)):
        for yr, refl in enumerate((r0, r1, r2, r3)):
            out[yr * 128 : yr * 128 + 128, :] = refl[...].reshape(128, 256)
        to = lax.rem(place[0] + k, X)
        at = pl.multiple_of(to * SBLK, SBLK)
        out[512:576, 0:128] = up[0, :, pl.ds(at, SBLK)]
        out[512:576, 128:256] = up[1, :, pl.ds(at, SBLK)]
        hit = jnp.max(jnp.where(recs == place[3] + to, 1.0, 0.0), axis=1, keepdims=True)
        rows = jnp.broadcast_to(hit, (8, 256))
        out[576:592, :] = jnp.concatenate([rows, rows], axis=0).astype(BF)


def wave_block(wave, y_src, half):
    parts = [wave[y_src * Z + 4 * half + q] for q in range(4)]
    real = jnp.concatenate([p[0:64] for p in parts], axis=0)
    imag = jnp.concatenate([p[64:128] for p in parts], axis=0)
    return jnp.concatenate([real, imag], axis=1)


def refl_block(refl, yr):
    return jnp.concatenate([r[yr * 128 : yr * 128 + 128, :] for r in refl], axis=0)


def residual_kernel(place, o0, o1, o2, o3, s0, s1, s2, s3, wave, res0, res1, res2, res3, other, high, low):
    my, mc = place[1], place[2]
    mine, theirs = (o0, o1, o2, o3), (s0, s1, s2, s3)
    acc = jnp.zeros((512, 256), F32)
    for yr in range(Y):
        y_src = lax.rem(my - yr + Y, Y)
        for refl, half in ((mine, mc), (theirs, 1 - mc)):
            acc += jnp.dot(
                refl_block(refl, yr), wave_block(wave, y_src, half), preferred_element_type=F32
            )
    for xr, (data, res) in enumerate(zip(mine, (res0, res1, res2, res3))):
        a = acc[xr * 128 : xr * 128 + 64]
        b = acc[xr * 128 + 64 : xr * 128 + 128]
        hits = data[576:592, 0:128].astype(F32)
        mask = jnp.concatenate(
            [jnp.broadcast_to(hits[r : r + 1], (RBLK, SBLK)) for r in range(8)], axis=0
        )
        real = mask * (a[:, :128] - b[:, 128:] - data[512:576, 0:128].astype(F32))
        imag = mask * (a[:, 128:] + b[:, :128] - data[512:576, 128:256].astype(F32))
        res[0] = real
        res[1] = imag
        top, bottom = slice(xr * 128, xr * 128 + 64), slice(xr * 128 + 64, xr * 128 + 128)
        rh, ih = real.astype(BF), imag.astype(BF)
        rl, il = (real - rh.astype(F32)).astype(BF), (imag - ih.astype(F32)).astype(BF)
        for out, re, im in ((high, rh, ih), (low, rl, il)):
            out[top, 0:128] = re
            out[top, 128:256] = im
            out[bottom, 0:128] = im
            out[bottom, 128:256] = -re
    refl_grad(my, 1 - mc, wave, high, low, other)


def refl_grad(my, half, wave, high, low, out):
    for yr in range(Y):
        w = wave_block(wave, lax.rem(my - yr + Y, Y), half)
        dims = (((1,), (1,)), ((), ()))
        g = lax.dot_general(high[...], w, dims, preferred_element_type=F32)
        g += lax.dot_general(low[...], w, dims, preferred_element_type=F32)
        out[yr] = g.reshape(X, 2, 64, 256)


def encode(value, out):
    rows = value.shape[0]
    most = jnp.max(jnp.abs(value), axis=0, keepdims=True)
    code = jnp.ceil(jnp.log2(jnp.maximum(most, 2.0**-100)) * 128.0 + 0.01)
    scaled = value * (jnp.exp2(code * (-1.0 / 128.0)) * 32767.0)
    scaled = jnp.clip(jnp.round(scaled), -32767.0, 32767.0)
    out[0:rows, :] = scaled.astype(jnp.int32).astype(jnp.int16)
    code = jnp.broadcast_to(code, (16, value.shape[1]))
    out[rows : rows + 16, :] = code.astype(jnp.int32).astype(jnp.int16)


def decode(coded):
    rows = coded.shape[0] - 16
    code = coded[rows : rows + 16, :].astype(jnp.int32).astype(F32)[0:1]
    scale = jnp.exp2(code * (1.0 / 128.0)) * (1.0 / 32767.0)
    return coded[0:rows, :].astype(jnp.int32).astype(F32) * scale


def grads_kernel(place, o0, o1, o2, o3, s0, s1, s2, s3, wave, high, low, out, own):
    my, mc = place[1], place[2]
    mine, theirs = (o0, o1, o2, o3), (s0, s1, s2, s3)
    for yr in range(Y):
        y_src = lax.rem(my - yr + Y, Y)
        for refl, half in ((mine, mc), (theirs, 1 - mc)):
            r = refl_block(refl, yr)
            dims = (((0,), (0,)), ((), ()))
            g = lax.dot_general(r, high[...], dims, preferred_element_type=F32)
            g += lax.dot_general(r, low[...], dims, preferred_element_type=F32)
            for q in range(4):
                part = g[q * 64 : q * 64 + 64]
                part = jnp.concatenate([part[:, 0:128], part[:, 128:256]], axis=0)
                encode(part, out.at[y_src * Z + 4 * half + q])
    refl_grad(my, mc, wave, high, low, own)


def core_sum_kernel(place, own, other, wave_part, s0, s1, s2, s3, wave_out):
    for xr in range(X):
        s0[xr] = (own[0, xr] + other[0, xr]).reshape(128, 256)
        for k, out in ((1, s1), (2, s2), (3, s3)):
            encode((own[k, xr] + other[k, xr]).reshape(128, 256), out.at[xr])


def y_sum_kernel(place, s0, s1, s2, s3, t0, t1, t2, t3):
    for k, out in enumerate((t0, t1, t2, t3)):
        total = s0[k] + decode(s1.at[k]) + decode(s2.at[k]) + decode(s3.at[k])
        if k:
            encode(total, out)
        else:
            out[...] = total


def x_sum_kernel(scale, place, t0, t1, t2, t3, out):
    total = t0[...] + decode(t1) + decode(t2) + decode(t3)
    out[...] = (total * scale).reshape(2, 64, 256)


def finish_kernel(scale, place, parts, r0, r1, r2, r3, wave_out, res_out):
    mx = place[0]
    for k in range(X):
        lanes = slice(k * SBLK, (k + 1) * SBLK)
        total = decode(parts.at[k * Z])
        for z in range(1, Z):
            total = total + decode(parts.at[k * Z + z])
        total = total * scale
        wave_out[0, :, lanes] = total[0:64]
        wave_out[1, :, lanes] = total[64:128]
    for k, piece in enumerate((r0, r1, r2, r3)):
        at = pl.multiple_of(lax.rem(mx + k, X) * SBLK, SBLK)
        for p in range(2):
            res_out[p, :, pl.ds(at, SBLK)] = piece[p]


def kernel_call(body, outs, ins, name, out_specs=None, aliases={}):
    return pl.pallas_call(
        body,
        out_shape=[jax.ShapeDtypeStruct(s, d) for s, d in outs],
        in_specs=[SMEM] + ins,
        out_specs=out_specs or [VMEM] * len(outs),
        input_output_aliases=aliases,
        compiler_params=PARAMS,
        name=name,
    )


def shards(reflectivity, downgoing, upgoing, recorded):
    mx, my, mc = lax.axis_index("x"), lax.axis_index("y"), lax.axis_index("c")
    place = jnp.stack([mx, my, mc, (my * C + mc) * X]).astype(jnp.int32)
    refl = reflectivity[:, 0]

    refl = [refl] + [send(refl, "y", Y, k) for k in range(1, Y)]
    wave, *mine = kernel_call(
        pack_kernel,
        [((X * Z, 128, 128), BF)] + [((592, 256), BF)] * X,
        [VMEM] * 7,
        "pack",
    )(place, *refl, downgoing[:, 0], upgoing[:, 0], recorded)
    wave = lax.all_to_all(wave, ("x", "z"), split_axis=0, concat_axis=0, tiled=True)
    mine = [mine[0]] + [send(mine[k], "x", X, k) for k in range(1, X)]
    theirs = [send(m, "c", C, 1) for m in mine]

    *pieces, other, high, low = kernel_call(
        residual_kernel,
        [((2, 64, 128), F32)] * X + [((Y, X, 2, 64, 256), F32)] + [((512, 256), BF)] * 2,
        [VMEM] * 9,
        "residual",
    )(place, *mine, *theirs, wave)
    other = send(other, "c", C, 1)
    wave_part, own = kernel_call(
        grads_kernel,
        [((X * Z, 144, 128), I16), ((Y, X, 2, 64, 256), F32)],
        [VMEM] * 11,
        "grads",
    )(place, *mine, *theirs, wave, high, low)
    *sums, wave_part = kernel_call(
        core_sum_kernel,
        [((X, 128, 256), F32)] + [((X, 144, 256), I16)] * 3 + [((X * Z, 144, 128), I16)],
        [VMEM, VMEM, ANY],
        "core_sum",
        out_specs=[VMEM] * Y + [ANY],
        aliases={3: Y},
    )(place, own, other, wave_part)
    pieces = [pieces[0]] + [send(pieces[k], "x", X, -k) for k in range(1, X)]
    sums = [sums[0]] + [send(sums[k], "y", Y, -k) for k in range(1, Y)]
    sums = kernel_call(
        y_sum_kernel, [((128, 256), F32)] + [((144, 256), I16)] * 3, [VMEM] * 4, "y_sum"
    )(place, *sums)
    sums = [sums[0]] + [send(sums[k], "x", X, -k) for k in range(1, X)]
    n_rec, n_src = Z * X * 64, Y * C * 512

    def x_sum(*refs):
        x_sum_kernel(n_src ** (-0.5), *refs)

    (grad_reflect,) = kernel_call(x_sum, [((2, 64, 256), F32)], [VMEM] * 4, "x_sum")(place, *sums)

    wave_part = lax.all_to_all(wave_part, ("x", "z"), split_axis=0, concat_axis=0, tiled=True)

    def finish(*refs):
        finish_kernel(n_rec ** (-0.5), *refs)

    grad_downgoing, residual = kernel_call(
        finish, [((2, 64, 512), F32), ((2, 64, 512), F32)], [VMEM] * 5, "finish"
    )(place, wave_part, *pieces)
    return residual[:, None], grad_reflect[:, None], grad_downgoing[:, None]


def solution(mesh):
    fine = Mesh(mesh.devices.reshape(X, Z, Y, C), ("x", "z", "y", "c"))
    spec = P(None, None, ("x", "z"), ("y", "c"))
    return jax.shard_map(
        shards,
        mesh=fine,
        in_specs=(spec, spec, spec, P(("x", "z"), None)),
        out_specs=(spec, spec, spec),
        check_vma=False,
    )
```

```python
import jax
import jax.numpy as jnp
from jax import lax
from jax.experimental import pallas as pl
from jax.experimental.pallas import tpu as pltpu
from jax.sharding import Mesh, PartitionSpec as P

RBLK = 8
SBLK = 128
X, Z, Y, C = 4, 8, 4, 2
BF, F32, I16 = jnp.bfloat16, jnp.float32, jnp.int16
VMEM = pl.BlockSpec(memory_space=pltpu.VMEM)
ANY = pl.BlockSpec(memory_space=pl.ANY)
SMEM = pl.BlockSpec(memory_space=pltpu.SMEM)
PARAMS = pltpu.CompilerParams(vmem_limit_bytes=16 * 1024 * 1024)


def send(value, axis, size, step):
    return lax.ppermute(value, axis, [(i, (i + step) % size) for i in range(size)])


def turn(value, pairs):
    moves = [(x * Y + y, to[0] * Y + to[1]) for (x, y), to in pairs.items()]
    return lax.ppermute(value, ("x", "y"), moves)


def pair_kernel(place, mine, theirs, out):
    out[place[2]] = mine[...].reshape(128, 256)
    out[1 - place[2]] = theirs[...].reshape(128, 256)


def after_kernel(place, refl, w1, w2, w6, w7, out):
    out[...] = refl[...]


def predict_kernel(place, *refs):
    rows, parts, (p0, p1, p2, p3, wave, refl, acc) = refs[:Y], refs[Y : Y + Z], refs[Y + Z :]
    mx, my, mz = place[0], place[1], place[3]
    for k, r in enumerate(rows):
        for c in range(C):
            refl[c, lax.rem(my - k + Y, Y)] = r[c]
    for zr, part in enumerate(parts):
        z = lax.rem(mz - zr + Z, Z)
        wave[z, :, 0:512] = part[0]
        wave[z, :, 512:1024] = part[1]
    total = jnp.zeros((512, 1024), F32)
    for c in range(C):
        w = wave[4 * c : 4 * c + 4].reshape(256, 1024)
        total += jnp.dot(refl[c].reshape(512, 256), w, preferred_element_type=F32)
    acc[...] = total.reshape(X, 128, 1024)
    for k, out in enumerate((p0, p1, p2, p3)):
        x = lax.rem(mx + k, X)
        a, b = acc[x, 0:64, :], acc[x, 64:128, :]
        real, imag = a[:, :512] - b[:, 512:], a[:, 512:] + b[:, :512]
        value = jnp.concatenate([real, imag], axis=0)
        if k:
            encode(value, out)
        else:
            out[...] = value


def residual_kernel(place, p0, p1, p2, p3, up, rec, res, coded):
    recs = rec[...]
    total = p0[...] + decode(p1) + decode(p2) + decode(p3)
    columns = []
    for k in range(X):
        hit = jnp.max(jnp.where(recs == place[4] + k, 1.0, 0.0), axis=1, keepdims=True)
        hit = jnp.broadcast_to(hit, (8, SBLK))
        columns.append(
            jnp.concatenate(
                [jnp.broadcast_to(hit[r : r + 1], (RBLK, SBLK)) for r in range(8)], axis=0
            )
        )
    mask = jnp.concatenate(columns, axis=1)
    parts = [mask * (total[64 * p : 64 * p + 64] - up[p].astype(F32)) for p in range(2)]
    res[0] = parts[0]
    res[1] = parts[1]
    encode(jnp.concatenate(parts, axis=0), coded)


def encode(value, out):
    rows = value.shape[0]
    most = jnp.max(jnp.abs(value), axis=0, keepdims=True)
    code = jnp.ceil(jnp.log2(jnp.maximum(most, 2.0**-100)) * 128.0 + 0.01)
    scaled = value * (jnp.exp2(code * (-1.0 / 128.0)) * 32767.0)
    scaled = jnp.clip(jnp.round(scaled), -32767.0, 32767.0)
    out[0:rows, :] = scaled.astype(jnp.int32).astype(jnp.int16)
    code = jnp.broadcast_to(code, (16, value.shape[1]))
    out[rows : rows + 16, :] = code.astype(jnp.int32).astype(jnp.int16)


def decode(coded):
    rows = coded.shape[0] - 16
    code = coded[rows : rows + 16, :].astype(jnp.int32).astype(F32)[0:1]
    scale = jnp.exp2(code * (1.0 / 128.0)) * (1.0 / 32767.0)
    return coded[0:rows, :].astype(jnp.int32).astype(F32) * scale


def grads_kernel(place, refl, wave, e0, e1, e2, e3, here, two, back, up, down, far, own, other, high, low, sums):
    mx, mc = place[0], place[2]
    for k, e in enumerate((e0, e1, e2, e3)):
        x = lax.rem(mx - k + X, X)
        value = decode(e)
        upper = value.astype(BF)
        lower = (value - upper.astype(F32)).astype(BF)
        for to, v in ((high, upper), (low, lower)):
            to[x, 0:64, 0:512] = v[0:64]
            to[x, 0:64, 512:1024] = v[64:128]
            to[x, 64:128, 0:512] = v[64:128]
            to[x, 64:128, 512:1024] = -v[0:64]
    h, l = high[...].reshape(512, 1024), low[...].reshape(512, 1024)
    for half in range(C):
        r = refl[half].reshape(512, 256)
        dims = (((0,), (0,)), ((), ()))
        g = lax.dot_general(r, h, dims, preferred_element_type=F32)
        g += lax.dot_general(r, l, dims, preferred_element_type=F32)
        for q in range(4):
            part = g[q * 64 : q * 64 + 64]
            part = jnp.concatenate([part[:, 0:512], part[:, 512:1024]], axis=0)
            sums[4 * half + q] = part
    def toward(step):
        return sums[lax.rem(place[3] + step + Z, Z)]

    here[...] = toward(0)
    two[...] = toward(2)
    back[...] = toward(-2)
    encode(toward(1), up.at[0])
    encode(toward(3), up.at[1])
    encode(toward(-1), down.at[0])
    encode(toward(-3), down.at[1])
    encode(toward(4), far)
    for to, half in ((own, mc), (other, 1 - mc)):
        w = wave[pl.ds(4 * half, 4)].reshape(256, 1024)
        dims = (((1,), (1,)), ((), ()))
        g = lax.dot_general(h, w, dims, preferred_element_type=F32)
        g += lax.dot_general(l, w, dims, preferred_element_type=F32)
        to[...] = g.reshape(X, 128, 256)


def core_sum_kernel(place, own, other, s0, s1, s2, s3):
    for k, out in enumerate((s0, s1, s2, s3)):
        x = lax.rem(place[1] + k, X)
        out[...] = own[x] + other[x]


def refl_sum_kernel(place, s0, s1, s2, s3, out):
    out[...] = (s0[...] + s1[...]) + (s2[...] + s3[...])


def relay_kernel(place, two, back, up, down, after, out_up, out_down):
    encode(two[...] + decode(up.at[1]), out_up)
    encode(back[...] + decode(down.at[1]), out_down)


def wave_sum_kernel(scale, place, here, up, down, up2, down2, far, out):
    total = here[...] + decode(up.at[0]) + decode(down.at[0]) + decode(up2) + decode(down2)
    total = total + decode(far)
    out[...] = (total * scale).reshape(2, 64, 512)


def kernel_call(body, outs, ins, name, out_specs=None, aliases={}, scratch=()):
    return pl.pallas_call(
        body,
        out_shape=[jax.ShapeDtypeStruct(s, d) for s, d in outs],
        in_specs=[SMEM] + ins,
        out_specs=out_specs or [VMEM] * len(outs),
        input_output_aliases=aliases,
        scratch_shapes=scratch,
        compiler_params=PARAMS,
        name=name,
    )


def shards(reflectivity, downgoing, upgoing, recorded):
    mx, my, mc = lax.axis_index("x"), lax.axis_index("y"), lax.axis_index("c")
    place = jnp.stack([mx, my, mc, lax.axis_index("z"), (my * C + mc) * X]).astype(jnp.int32)
    n_rec, n_src = Z * X * 64, Y * C * 512
    grid = [(x, y) for x in range(X) for y in range(Y)]

    wave = {0: downgoing[:, 0]}
    wave |= {k % Z: send(wave[0], "z", Z, k) for k in (2, -2, 1, -1)}
    wave[3] = send(wave[2], "z", Z, 1)
    wave[5] = send(wave[6], "z", Z, -1)
    wave[4] = send(wave[2], "z", Z, 2)
    wave = [wave[k] for k in range(Z)]
    refl = reflectivity[:, 0]
    (refl,) = kernel_call(pair_kernel, [((C, 128, 256), BF)], [VMEM] * 2, "pair")(
        place, refl, send(refl, "c", C, 1)
    )
    refl = turn(refl, {(x, y): (y, x) for x, y in grid})
    (refl,) = kernel_call(after_kernel, [((C, 128, 256), BF)], [VMEM] + [ANY] * 4, "after")(
        place, refl, wave[1], wave[2], wave[6], wave[7]
    )
    refl = [refl] + [send(refl, "y", Y, k) for k in range(1, Y)]

    *pred, wave, refl = kernel_call(
        predict_kernel,
        [((128, 512), F32)] + [((144, 512), I16)] * 3 + [((Z, 64, 1024), BF), ((C, X, 128, 256), BF)],
        [VMEM] * 12,
        "predict",
        scratch=[pltpu.VMEM((X, 128, 1024), F32)],
    )(place, *refl, *wave)
    pred = [pred[0]] + [send(pred[k], "x", X, k) for k in range(1, X)]
    residual, coded = kernel_call(
        residual_kernel, [((2, 64, 512), F32), ((144, 512), I16)], [VMEM] * 6, "residual"
    )(place, *pred, upgoing[:, 0], recorded)
    coded = [coded] + [send(coded, "x", X, k) for k in range(1, X)]
    here, two, back, up, down, far, own, other = kernel_call(
        grads_kernel,
        [((128, 512), F32)] * 3
        + [((2, 144, 512), I16)] * 2
        + [((144, 512), I16)]
        + [((X, 128, 256), F32)] * 2,
        [VMEM] * 6,
        "grads",
        scratch=[pltpu.VMEM((X, 128, 1024), BF)] * 2 + [pltpu.VMEM((Z, 128, 512), F32)],
    )(place, refl, wave, *coded)
    up, down, far = send(up, "z", Z, 1), send(down, "z", Z, -1), send(far, "z", Z, 4)
    other = send(other, "c", C, 1)
    sums = kernel_call(core_sum_kernel, [((128, 256), F32)] * X, [VMEM] * 2, "core_sum")(
        place, own, other
    )
    up2, down2 = kernel_call(relay_kernel, [((144, 512), I16)] * 2, [VMEM] * 4 + [ANY], "relay")(
        place, two, back, up, down, sums[0]
    )
    up2, down2 = send(up2, "z", Z, 2), send(down2, "z", Z, -2)

    sums = [sums[0]] + [send(sums[k], "y", Y, k) for k in range(1, Y)]

    def wave_sum(*refs):
        wave_sum_kernel(n_rec ** (-0.5), *refs)

    (grad,) = kernel_call(refl_sum_kernel, [((128, 256), F32)], [VMEM] * 4, "refl_sum")(
        place, *sums
    )
    grad = turn(grad, {(x, y): (y, x) for x, y in grid})
    (grad_downgoing,) = kernel_call(wave_sum, [((2, 64, 512), F32)], [VMEM] * 6, "wave_sum")(
        place, here, up, down, up2, down2, far
    )
    grad_reflect = grad.reshape(2, 64, 256) * n_src ** (-0.5)
    return residual[:, None], grad_reflect[:, None], grad_downgoing[:, None]


def solution(mesh):
    fine = Mesh(mesh.devices.reshape(X, Z, Y, C), ("x", "z", "y", "c"))
    spec = P(None, None, ("x", "z"), ("y", "c"))
    return jax.shard_map(
        shards,
        mesh=fine,
        in_specs=(spec, spec, spec, P(("x", "z"), None)),
        out_specs=(spec, spec, spec),
        check_vma=False,
    )
```

```python
import jax
import jax.numpy as jnp
from jax import lax
from jax.experimental import pallas as pl
from jax.experimental.pallas import tpu as pltpu
from jax.sharding import Mesh, PartitionSpec as P

RBLK = 8
SBLK = 128
X, Z, Y, C = 4, 8, 4, 2
BF, F32, I16 = jnp.bfloat16, jnp.float32, jnp.int16
VMEM = pl.BlockSpec(memory_space=pltpu.VMEM)
ANY = pl.BlockSpec(memory_space=pl.ANY)
SMEM = pl.BlockSpec(memory_space=pltpu.SMEM)
PARAMS = pltpu.CompilerParams(vmem_limit_bytes=16 * 1024 * 1024)


def send(value, axis, size, step):
    return lax.ppermute(value, axis, [(i, (i + step) % size) for i in range(size)])


def turn(value, pairs):
    moves = [(x * Y + y, to[0] * Y + to[1]) for (x, y), to in pairs.items()]
    return lax.ppermute(value, ("x", "y"), moves)


def pair_kernel(place, mine, theirs, out):
    out[place[2]] = mine[...].reshape(128, 256)
    out[1 - place[2]] = theirs[...].reshape(128, 256)


def predict_kernel(place, *refs):
    rows, parts, (p0, p1, p2, p3, wave, refl, acc) = refs[:Y], refs[Y : Y + Z], refs[Y + Z :]
    mx, my, mz = place[0], place[1], place[3]
    for k, r in enumerate(rows):
        for c in range(C):
            refl[c, lax.rem(my - k + Y, Y)] = r[c]
    for zr, part in enumerate(parts):
        z = lax.rem(mz - zr + Z, Z)
        wave[z, :, 0:512] = part[0]
        wave[z, :, 512:1024] = part[1]
    total = jnp.zeros((512, 1024), F32)
    for c in range(C):
        w = wave[4 * c : 4 * c + 4].reshape(256, 1024)
        total += jnp.dot(refl[c].reshape(512, 256), w, preferred_element_type=F32)
    acc[...] = total.reshape(X, 128, 1024)
    for k, out in enumerate((p0, p1, p2, p3)):
        x = lax.rem(mx + k, X)
        a, b = acc[x, 0:64, :], acc[x, 64:128, :]
        real, imag = a[:, :512] - b[:, 512:], a[:, 512:] + b[:, :512]
        value = jnp.concatenate([real, imag], axis=0)
        if k:
            encode(value, out)
        else:
            out[...] = value


def residual_kernel(place, p0, p1, p2, p3, up, rec, res, coded):
    recs = rec[...]
    total = p0[...] + decode(p1) + decode(p2) + decode(p3)
    columns = []
    for k in range(X):
        hit = jnp.max(jnp.where(recs == place[4] + k, 1.0, 0.0), axis=1, keepdims=True)
        hit = jnp.broadcast_to(hit, (8, SBLK))
        columns.append(
            jnp.concatenate(
                [jnp.broadcast_to(hit[r : r + 1], (RBLK, SBLK)) for r in range(8)], axis=0
            )
        )
    mask = jnp.concatenate(columns, axis=1)
    parts = [mask * (total[64 * p : 64 * p + 64] - up[p].astype(F32)) for p in range(2)]
    res[0] = parts[0]
    res[1] = parts[1]
    encode(jnp.concatenate(parts, axis=0), coded)


def encode(value, out):
    rows = value.shape[0]
    most = jnp.max(jnp.abs(value), axis=0, keepdims=True)
    code = jnp.ceil(jnp.log2(jnp.maximum(most, 2.0**-100)) * 128.0 + 0.01)
    scaled = value * (jnp.exp2(code * (-1.0 / 128.0)) * 32767.0)
    scaled = jnp.clip(jnp.round(scaled), -32767.0, 32767.0)
    out[0:rows, :] = scaled.astype(jnp.int32).astype(jnp.int16)
    code = jnp.broadcast_to(code, (16, value.shape[1]))
    out[rows : rows + 16, :] = code.astype(jnp.int32).astype(jnp.int16)


def decode(coded):
    rows = coded.shape[0] - 16
    code = coded[rows : rows + 16, :].astype(jnp.int32).astype(F32)[0:1]
    scale = jnp.exp2(code * (1.0 / 128.0)) * (1.0 / 32767.0)
    return coded[0:rows, :].astype(jnp.int32).astype(F32) * scale


def grads_kernel(place, refl, wave, e0, e1, e2, e3, here, two, back, up, down, far, own, other, high, low, sums):
    mx, mc = place[0], place[2]
    for k, e in enumerate((e0, e1, e2, e3)):
        x = lax.rem(mx - k + X, X)
        value = decode(e)
        upper = value.astype(BF)
        lower = (value - upper.astype(F32)).astype(BF)
        for to, v in ((high, upper), (low, lower)):
            to[x, 0:64, 0:512] = v[0:64]
            to[x, 0:64, 512:1024] = v[64:128]
            to[x, 64:128, 0:512] = v[64:128]
            to[x, 64:128, 512:1024] = -v[0:64]
    h, l = high[...].reshape(512, 1024), low[...].reshape(512, 1024)
    for half in range(C):
        r = refl[half].reshape(512, 256)
        dims = (((0,), (0,)), ((), ()))
        g = lax.dot_general(r, h, dims, preferred_element_type=F32)
        g += lax.dot_general(r, l, dims, preferred_element_type=F32)
        for q in range(4):
            part = g[q * 64 : q * 64 + 64]
            part = jnp.concatenate([part[:, 0:512], part[:, 512:1024]], axis=0)
            sums[4 * half + q] = part
    def toward(step):
        return sums[lax.rem(place[3] + step + Z, Z)]

    here[...] = toward(0)
    two[...] = toward(2)
    back[...] = toward(-2)
    encode(toward(1), up.at[0])
    encode(toward(3), up.at[1])
    encode(toward(-1), down.at[0])
    encode(toward(-3), down.at[1])
    encode(toward(4), far)
    for to, half in ((own, mc), (other, 1 - mc)):
        w = wave[pl.ds(4 * half, 4)].reshape(256, 1024)
        dims = (((1,), (1,)), ((), ()))
        g = lax.dot_general(h, w, dims, preferred_element_type=F32)
        g += lax.dot_general(l, w, dims, preferred_element_type=F32)
        to[...] = g.reshape(X, 128, 256)


def core_sum_kernel(place, own, other, s0, s1, s2, s3):
    for k, out in enumerate((s0, s1, s2, s3)):
        x = lax.rem(place[1] + k, X)
        out[...] = own[x] + other[x]


def refl_sum_kernel(place, s0, s1, s2, s3, out):
    out[...] = (s0[...] + s1[...]) + (s2[...] + s3[...])


def relay_kernel(place, two, back, up, down, after, out_up, out_down):
    encode(two[...] + decode(up.at[1]), out_up)
    encode(back[...] + decode(down.at[1]), out_down)


def wave_sum_kernel(scale, place, here, up, down, up2, down2, far, out):
    total = here[...] + decode(up.at[0]) + decode(down.at[0]) + decode(up2) + decode(down2)
    total = total + decode(far)
    out[...] = (total * scale).reshape(2, 64, 512)


def kernel_call(body, outs, ins, name, out_specs=None, aliases={}, scratch=()):
    return pl.pallas_call(
        body,
        out_shape=[jax.ShapeDtypeStruct(s, d) for s, d in outs],
        in_specs=[SMEM] + ins,
        out_specs=out_specs or [VMEM] * len(outs),
        input_output_aliases=aliases,
        scratch_shapes=scratch,
        compiler_params=PARAMS,
        name=name,
    )


def shards(reflectivity, downgoing, upgoing, recorded):
    mx, my, mc = lax.axis_index("x"), lax.axis_index("y"), lax.axis_index("c")
    place = jnp.stack([mx, my, mc, lax.axis_index("z"), (my * C + mc) * X]).astype(jnp.int32)
    n_rec, n_src = Z * X * 64, Y * C * 512
    grid = [(x, y) for x in range(X) for y in range(Y)]

    wave = {0: downgoing[:, 0]}
    wave |= {k % Z: send(wave[0], "z", Z, k) for k in (2, -2, 1, -1)}
    wave[3] = send(wave[2], "z", Z, 1)
    wave[5] = send(wave[6], "z", Z, -1)
    wave[4] = send(wave[2], "z", Z, 2)
    wave = [wave[k] for k in range(Z)]
    refl = reflectivity[:, 0]
    (refl,) = kernel_call(pair_kernel, [((C, 128, 256), BF)], [VMEM] * 2, "pair")(
        place, refl, send(refl, "c", C, 1)
    )
    refl = turn(refl, {(x, y): (y, x) for x, y in grid})
    refl = [refl] + [send(refl, "y", Y, k) for k in range(1, Y)]

    *pred, wave, refl = kernel_call(
        predict_kernel,
        [((128, 512), F32)] + [((144, 512), I16)] * 3 + [((Z, 64, 1024), BF), ((C, X, 128, 256), BF)],
        [VMEM] * 12,
        "predict",
        scratch=[pltpu.VMEM((X, 128, 1024), F32)],
    )(place, *refl, *wave)
    pred = [pred[0]] + [send(pred[k], "x", X, k) for k in range(1, X)]
    residual, coded = kernel_call(
        residual_kernel, [((2, 64, 512), F32), ((144, 512), I16)], [VMEM] * 6, "residual"
    )(place, *pred, upgoing[:, 0], recorded)
    coded = [coded] + [send(coded, "x", X, k) for k in range(1, X)]
    here, two, back, up, down, far, own, other = kernel_call(
        grads_kernel,
        [((128, 512), F32)] * 3
        + [((2, 144, 512), I16)] * 2
        + [((144, 512), I16)]
        + [((X, 128, 256), F32)] * 2,
        [VMEM] * 6,
        "grads",
        scratch=[pltpu.VMEM((X, 128, 1024), BF)] * 2 + [pltpu.VMEM((Z, 128, 512), F32)],
    )(place, refl, wave, *coded)
    up, down, far = send(up, "z", Z, 1), send(down, "z", Z, -1), send(far, "z", Z, 4)
    other = send(other, "c", C, 1)
    sums = kernel_call(core_sum_kernel, [((128, 256), F32)] * X, [VMEM] * 2, "core_sum")(
        place, own, other
    )
    up2, down2 = kernel_call(relay_kernel, [((144, 512), I16)] * 2, [VMEM] * 4 + [ANY], "relay")(
        place, two, back, up, down, sums[0]
    )
    up2, down2 = send(up2, "z", Z, 2), send(down2, "z", Z, -2)

    sums = [sums[0]] + [send(sums[k], "y", Y, k) for k in range(1, Y)]

    def wave_sum(*refs):
        wave_sum_kernel(n_rec ** (-0.5), *refs)

    (grad,) = kernel_call(refl_sum_kernel, [((128, 256), F32)], [VMEM] * 4, "refl_sum")(
        place, *sums
    )
    grad = turn(grad, {(x, y): (y, x) for x, y in grid})
    (grad_downgoing,) = kernel_call(wave_sum, [((2, 64, 512), F32)], [VMEM] * 6, "wave_sum")(
        place, here, up, down, up2, down2, far
    )
    grad_reflect = grad.reshape(2, 64, 256) * n_src ** (-0.5)
    return residual[:, None], grad_reflect[:, None], grad_downgoing[:, None]


def solution(mesh):
    fine = Mesh(mesh.devices.reshape(X, Z, Y, C), ("x", "z", "y", "c"))
    spec = P(None, None, ("x", "z"), ("y", "c"))
    return jax.shard_map(
        shards,
        mesh=fine,
        in_specs=(spec, spec, spec, P(("x", "z"), None)),
        out_specs=(spec, spec, spec),
        check_vma=False,
    )
```

```python
import jax
import jax.numpy as jnp
from jax import lax
from jax.experimental import pallas as pl
from jax.experimental.pallas import tpu as pltpu
from jax.sharding import Mesh, PartitionSpec as P

RBLK = 8
SBLK = 128
X, Z, Y, C = 4, 8, 4, 2
BF, F32, I16 = jnp.bfloat16, jnp.float32, jnp.int16
VMEM = pl.BlockSpec(memory_space=pltpu.VMEM)
ANY = pl.BlockSpec(memory_space=pl.ANY)
SMEM = pl.BlockSpec(memory_space=pltpu.SMEM)
PARAMS = pltpu.CompilerParams(vmem_limit_bytes=16 * 1024 * 1024)


def send(value, axis, size, step):
    return lax.ppermute(value, axis, [(i, (i + step) % size) for i in range(size)])


def turn(value, pairs):
    moves = [(x * Y + y, to[0] * Y + to[1]) for (x, y), to in pairs.items()]
    return lax.ppermute(value, ("x", "y"), moves)


def pair_kernel(place, mine, theirs, out):
    out[place[2]] = mine[...].reshape(128, 256)
    out[1 - place[2]] = theirs[...].reshape(128, 256)


def predict_kernel(place, *refs):
    rows, parts, (p0, p1, p2, p3, wave, refl, acc) = refs[:Y], refs[Y : Y + Z], refs[Y + Z :]
    mx, my, mz = place[0], place[1], place[3]
    for k, r in enumerate(rows):
        for c in range(C):
            refl[c, lax.rem(my - k + Y, Y)] = r[c]
    for zr, part in enumerate(parts):
        z = lax.rem(mz - zr + Z, Z)
        wave[z, :, 0:512] = part[0]
        wave[z, :, 512:1024] = part[1]
    total = jnp.zeros((512, 1024), F32)
    for c in range(C):
        w = wave[4 * c : 4 * c + 4].reshape(256, 1024)
        total += jnp.dot(refl[c].reshape(512, 256), w, preferred_element_type=F32)
    acc[...] = total.reshape(X, 128, 1024)
    for k, out in enumerate((p0, p1, p2, p3)):
        x = lax.rem(mx + k, X)
        a, b = acc[x, 0:64, :], acc[x, 64:128, :]
        out[0:64, :] = a[:, :512] - b[:, 512:]
        out[64:128, :] = a[:, 512:] + b[:, :512]


def residual_kernel(place, p0, p1, p2, p3, up, rec, res, coded):
    recs = rec[...]
    total = (p0[...] + p1[...]) + (p2[...] + p3[...])
    columns = []
    for k in range(X):
        hit = jnp.max(jnp.where(recs == place[4] + k, 1.0, 0.0), axis=1, keepdims=True)
        hit = jnp.broadcast_to(hit, (8, SBLK))
        columns.append(
            jnp.concatenate(
                [jnp.broadcast_to(hit[r : r + 1], (RBLK, SBLK)) for r in range(8)], axis=0
            )
        )
    mask = jnp.concatenate(columns, axis=1)
    parts = [mask * (total[64 * p : 64 * p + 64] - up[p].astype(F32)) for p in range(2)]
    res[0] = parts[0]
    res[1] = parts[1]
    encode(jnp.concatenate(parts, axis=0), coded)


def encode(value, out):
    rows = value.shape[0]
    most = jnp.max(jnp.abs(value), axis=0, keepdims=True)
    code = jnp.ceil(jnp.log2(jnp.maximum(most, 2.0**-100)) * 128.0 + 0.01)
    scaled = value * (jnp.exp2(code * (-1.0 / 128.0)) * 32767.0)
    scaled = jnp.clip(jnp.round(scaled), -32767.0, 32767.0)
    out[0:rows, :] = scaled.astype(jnp.int32).astype(jnp.int16)
    code = jnp.broadcast_to(code, (16, value.shape[1]))
    out[rows : rows + 16, :] = code.astype(jnp.int32).astype(jnp.int16)


def decode(coded):
    rows = coded.shape[0] - 16
    code = coded[rows : rows + 16, :].astype(jnp.int32).astype(F32)[0:1]
    scale = jnp.exp2(code * (1.0 / 128.0)) * (1.0 / 32767.0)
    return coded[0:rows, :].astype(jnp.int32).astype(F32) * scale


def grads_kernel(place, refl, wave, e0, e1, e2, e3, here, two, back, up, down, far, own, other, high, low, sums):
    mx, mc = place[0], place[2]
    for k, e in enumerate((e0, e1, e2, e3)):
        x = lax.rem(mx - k + X, X)
        value = decode(e)
        upper = value.astype(BF)
        lower = (value - upper.astype(F32)).astype(BF)
        for to, v in ((high, upper), (low, lower)):
            to[x, 0:64, 0:512] = v[0:64]
            to[x, 0:64, 512:1024] = v[64:128]
            to[x, 64:128, 0:512] = v[64:128]
            to[x, 64:128, 512:1024] = -v[0:64]
    h, l = high[...].reshape(512, 1024), low[...].reshape(512, 1024)
    for half in range(C):
        r = refl[half].reshape(512, 256)
        dims = (((0,), (0,)), ((), ()))
        g = lax.dot_general(r, h, dims, preferred_element_type=F32)
        g += lax.dot_general(r, l, dims, preferred_element_type=F32)
        for q in range(4):
            part = g[q * 64 : q * 64 + 64]
            part = jnp.concatenate([part[:, 0:512], part[:, 512:1024]], axis=0)
            sums[4 * half + q] = part
    def toward(step):
        return sums[lax.rem(place[3] + step + Z, Z)]

    here[...] = toward(0)
    two[...] = toward(2)
    back[...] = toward(-2)
    encode(toward(1), up.at[0])
    encode(toward(3), up.at[1])
    encode(toward(-1), down.at[0])
    encode(toward(-3), down.at[1])
    encode(toward(4), far)
    for to, half in ((own, mc), (other, 1 - mc)):
        w = wave[pl.ds(4 * half, 4)].reshape(256, 1024)
        dims = (((1,), (1,)), ((), ()))
        g = lax.dot_general(h, w, dims, preferred_element_type=F32)
        g += lax.dot_general(l, w, dims, preferred_element_type=F32)
        to[...] = g.reshape(X, 128, 256)


def core_sum_kernel(place, own, other, s0, s1, s2, s3):
    for k, out in enumerate((s0, s1, s2, s3)):
        x = lax.rem(place[1] + k, X)
        out[...] = own[x] + other[x]


def refl_sum_kernel(place, s0, s1, s2, s3, out):
    out[...] = (s0[...] + s1[...]) + (s2[...] + s3[...])


def relay_kernel(place, two, back, up, down, after, out_up, out_down):
    encode(two[...] + decode(up.at[1]), out_up)
    encode(back[...] + decode(down.at[1]), out_down)


def wave_sum_kernel(scale, place, here, up, down, up2, down2, far, out):
    total = here[...] + decode(up.at[0]) + decode(down.at[0]) + decode(up2) + decode(down2)
    total = total + decode(far)
    out[...] = (total * scale).reshape(2, 64, 512)


def kernel_call(body, outs, ins, name, out_specs=None, aliases={}, scratch=()):
    return pl.pallas_call(
        body,
        out_shape=[jax.ShapeDtypeStruct(s, d) for s, d in outs],
        in_specs=[SMEM] + ins,
        out_specs=out_specs or [VMEM] * len(outs),
        input_output_aliases=aliases,
        scratch_shapes=scratch,
        compiler_params=PARAMS,
        name=name,
    )


def shards(reflectivity, downgoing, upgoing, recorded):
    mx, my, mc = lax.axis_index("x"), lax.axis_index("y"), lax.axis_index("c")
    place = jnp.stack([mx, my, mc, lax.axis_index("z"), (my * C + mc) * X]).astype(jnp.int32)
    n_rec, n_src = Z * X * 64, Y * C * 512
    grid = [(x, y) for x in range(X) for y in range(Y)]

    wave = {0: downgoing[:, 0]}
    wave |= {k % Z: send(wave[0], "z", Z, k) for k in (2, -2, 1, -1)}
    wave[3] = send(wave[2], "z", Z, 1)
    wave[5] = send(wave[6], "z", Z, -1)
    wave[4] = send(wave[2], "z", Z, 2)
    wave = [wave[k] for k in range(Z)]
    refl = reflectivity[:, 0]
    (refl,) = kernel_call(pair_kernel, [((C, 128, 256), BF)], [VMEM] * 2, "pair")(
        place, refl, send(refl, "c", C, 1)
    )
    refl = turn(refl, {(x, y): (y, x) for x, y in grid})
    refl = [refl] + [send(refl, "y", Y, k) for k in range(1, Y)]

    *pred, wave, refl = kernel_call(
        predict_kernel,
        [((128, 512), F32)] * X + [((Z, 64, 1024), BF), ((C, X, 128, 256), BF)],
        [VMEM] * 12,
        "predict",
        scratch=[pltpu.VMEM((X, 128, 1024), F32)],
    )(place, *refl, *wave)
    pred = [pred[0]] + [send(pred[k], "x", X, k) for k in range(1, X)]
    residual, coded = kernel_call(
        residual_kernel, [((2, 64, 512), F32), ((144, 512), I16)], [VMEM] * 6, "residual"
    )(place, *pred, upgoing[:, 0], recorded)
    coded = [coded] + [send(coded, "x", X, k) for k in range(1, X)]
    here, two, back, up, down, far, own, other = kernel_call(
        grads_kernel,
        [((128, 512), F32)] * 3
        + [((2, 144, 512), I16)] * 2
        + [((144, 512), I16)]
        + [((X, 128, 256), F32)] * 2,
        [VMEM] * 6,
        "grads",
        scratch=[pltpu.VMEM((X, 128, 1024), BF)] * 2 + [pltpu.VMEM((Z, 128, 512), F32)],
    )(place, refl, wave, *coded)
    up, down, far = send(up, "z", Z, 1), send(down, "z", Z, -1), send(far, "z", Z, 4)
    other = send(other, "c", C, 1)
    sums = kernel_call(core_sum_kernel, [((128, 256), F32)] * X, [VMEM] * 2, "core_sum")(
        place, own, other
    )
    up2, down2 = kernel_call(relay_kernel, [((144, 512), I16)] * 2, [VMEM] * 4 + [ANY], "relay")(
        place, two, back, up, down, sums[0]
    )
    up2, down2 = send(up2, "z", Z, 2), send(down2, "z", Z, -2)

    sums = [sums[0]] + [send(sums[k], "y", Y, k) for k in range(1, Y)]

    def wave_sum(*refs):
        wave_sum_kernel(n_rec ** (-0.5), *refs)

    (grad,) = kernel_call(refl_sum_kernel, [((128, 256), F32)], [VMEM] * 4, "refl_sum")(
        place, *sums
    )
    grad = turn(grad, {(x, y): (y, x) for x, y in grid})
    (grad_downgoing,) = kernel_call(wave_sum, [((2, 64, 512), F32)], [VMEM] * 6, "wave_sum")(
        place, here, up, down, up2, down2, far
    )
    grad_reflect = grad.reshape(2, 64, 256) * n_src ** (-0.5)
    return residual[:, None], grad_reflect[:, None], grad_downgoing[:, None]


def solution(mesh):
    fine = Mesh(mesh.devices.reshape(X, Z, Y, C), ("x", "z", "y", "c"))
    spec = P(None, None, ("x", "z"), ("y", "c"))
    return jax.shard_map(
        shards,
        mesh=fine,
        in_specs=(spec, spec, spec, P(("x", "z"), None)),
        out_specs=(spec, spec, spec),
        check_vma=False,
    )
```

```python
import jax
import jax.numpy as jnp
from jax import lax
from jax.experimental import pallas as pl
from jax.experimental.pallas import tpu as pltpu
from jax.sharding import Mesh, PartitionSpec as P

RBLK = 8
SBLK = 128
X, Z, Y, C = 4, 8, 4, 2
BF, F32, I16 = jnp.bfloat16, jnp.float32, jnp.int16
VMEM = pl.BlockSpec(memory_space=pltpu.VMEM)
ANY = pl.BlockSpec(memory_space=pl.ANY)
SMEM = pl.BlockSpec(memory_space=pltpu.SMEM)
PARAMS = pltpu.CompilerParams(vmem_limit_bytes=16 * 1024 * 1024)


def send(value, axis, size, step):
    return lax.ppermute(value, axis, [(i, (i + step) % size) for i in range(size)])


def turn(value, pairs):
    moves = [(x * Y + y, to[0] * Y + to[1]) for (x, y), to in pairs.items()]
    return lax.ppermute(value, ("x", "y"), moves)


def pair_kernel(place, mine, theirs, out):
    out[place[2]] = mine[...].reshape(128, 256)
    out[1 - place[2]] = theirs[...].reshape(128, 256)


def predict_kernel(place, *refs):
    rows, parts, (p0, p1, p2, p3, wave, refl, acc) = refs[:Y], refs[Y : Y + Z], refs[Y + Z :]
    mx, my, mz = place[0], place[1], place[3]
    for k, r in enumerate(rows):
        for c in range(C):
            refl[c, lax.rem(my - k + Y, Y)] = r[c]
    for zr, part in enumerate(parts):
        z = lax.rem(mz - zr + Z, Z)
        wave[z, :, 0:512] = part[0]
        wave[z, :, 512:1024] = part[1]
    total = jnp.zeros((512, 1024), F32)
    for c in range(C):
        w = wave[4 * c : 4 * c + 4].reshape(256, 1024)
        total += jnp.dot(refl[c].reshape(512, 256), w, preferred_element_type=F32)
    acc[...] = total.reshape(X, 128, 1024)
    for k, out in enumerate((p0, p1, p2, p3)):
        x = lax.rem(mx + k, X)
        a, b = acc[x, 0:64, :], acc[x, 64:128, :]
        real, imag = a[:, :512] - b[:, 512:], a[:, 512:] + b[:, :512]
        value = jnp.concatenate([real, imag], axis=0)
        if k:
            encode(value, out)
        else:
            out[...] = value


def residual_kernel(place, p0, p1, p2, p3, up, rec, res, coded):
    recs = rec[...]
    total = p0[...] + decode(p1) + decode(p2) + decode(p3)
    columns = []
    for k in range(X):
        hit = jnp.max(jnp.where(recs == place[4] + k, 1.0, 0.0), axis=1, keepdims=True)
        hit = jnp.broadcast_to(hit, (8, SBLK))
        columns.append(
            jnp.concatenate(
                [jnp.broadcast_to(hit[r : r + 1], (RBLK, SBLK)) for r in range(8)], axis=0
            )
        )
    mask = jnp.concatenate(columns, axis=1)
    parts = [mask * (total[64 * p : 64 * p + 64] - up[p].astype(F32)) for p in range(2)]
    res[0] = parts[0]
    res[1] = parts[1]
    encode(jnp.concatenate(parts, axis=0), coded)


def encode(value, out):
    rows = value.shape[0]
    most = jnp.max(jnp.abs(value), axis=0, keepdims=True)
    code = jnp.ceil(jnp.log2(jnp.maximum(most, 2.0**-100)) * 128.0 + 0.01)
    scaled = value * (jnp.exp2(code * (-1.0 / 128.0)) * 32767.0)
    scaled = jnp.clip(jnp.round(scaled), -32767.0, 32767.0)
    out[0:rows, :] = scaled.astype(jnp.int32).astype(jnp.int16)
    code = jnp.broadcast_to(code, (16, value.shape[1]))
    out[rows : rows + 16, :] = code.astype(jnp.int32).astype(jnp.int16)


def decode(coded):
    rows = coded.shape[0] - 16
    code = coded[rows : rows + 16, :].astype(jnp.int32).astype(F32)[0:1]
    scale = jnp.exp2(code * (1.0 / 128.0)) * (1.0 / 32767.0)
    return coded[0:rows, :].astype(jnp.int32).astype(F32) * scale


def grads_kernel(place, refl, wave, e0, e1, e2, e3, here, two, back, up, down, far, own, other, high, low, sums):
    mx, mc = place[0], place[2]
    for k, e in enumerate((e0, e1, e2, e3)):
        x = lax.rem(mx - k + X, X)
        value = decode(e)
        upper = value.astype(BF)
        lower = (value - upper.astype(F32)).astype(BF)
        for to, v in ((high, upper), (low, lower)):
            to[x, 0:64, 0:512] = v[0:64]
            to[x, 0:64, 512:1024] = v[64:128]
            to[x, 64:128, 0:512] = v[64:128]
            to[x, 64:128, 512:1024] = -v[0:64]
    h, l = high[...].reshape(512, 1024), low[...].reshape(512, 1024)
    for half in range(C):
        r = refl[half].reshape(512, 256)
        dims = (((0,), (0,)), ((), ()))
        g = lax.dot_general(r, h, dims, preferred_element_type=F32)
        g += lax.dot_general(r, l, dims, preferred_element_type=F32)
        for q in range(4):
            part = g[q * 64 : q * 64 + 64]
            part = jnp.concatenate([part[:, 0:512], part[:, 512:1024]], axis=0)
            sums[4 * half + q] = part
    def toward(step):
        return sums[lax.rem(place[3] + step + Z, Z)]

    here[...] = toward(0)
    two[...] = toward(2)
    back[...] = toward(-2)
    encode(toward(1), up.at[0])
    encode(toward(3), up.at[1])
    encode(toward(-1), down.at[0])
    encode(toward(-3), down.at[1])
    encode(toward(4), far)
    for to, half in ((own, mc), (other, 1 - mc)):
        w = wave[pl.ds(4 * half, 4)].reshape(256, 1024)
        dims = (((1,), (1,)), ((), ()))
        g = lax.dot_general(h, w, dims, preferred_element_type=F32)
        g += lax.dot_general(l, w, dims, preferred_element_type=F32)
        to[...] = g.reshape(X, 128, 256)


def core_sum_kernel(place, own, other, s0, s1, s2, s3):
    for k, out in enumerate((s0, s1, s2, s3)):
        x = lax.rem(place[1] + k, X)
        out[...] = own[x] + other[x]


def refl_sum_kernel(place, s0, s1, s2, s3, here, up, down, out, base):
    out[...] = (s0[...] + s1[...]) + (s2[...] + s3[...])
    base[...] = here[...] + decode(up.at[0]) + decode(down.at[0])


def relay_kernel(place, two, back, up, down, after, out_up, out_down):
    encode(two[...] + decode(up.at[1]), out_up)
    encode(back[...] + decode(down.at[1]), out_down)


def last_kernel(scale, refl_scale, place, base, up2, down2, far, grad, out, refl_out):
    total = base[...] + decode(up2) + decode(down2) + decode(far)
    out[...] = (total * scale).reshape(2, 64, 512)
    refl_out[...] = (grad[...] * refl_scale).reshape(2, 64, 256)


def kernel_call(body, outs, ins, name, out_specs=None, aliases={}, scratch=()):
    return pl.pallas_call(
        body,
        out_shape=[jax.ShapeDtypeStruct(s, d) for s, d in outs],
        in_specs=[SMEM] + ins,
        out_specs=out_specs or [VMEM] * len(outs),
        input_output_aliases=aliases,
        scratch_shapes=scratch,
        compiler_params=PARAMS,
        name=name,
    )


def shards(reflectivity, downgoing, upgoing, recorded):
    mx, my, mc = lax.axis_index("x"), lax.axis_index("y"), lax.axis_index("c")
    place = jnp.stack([mx, my, mc, lax.axis_index("z"), (my * C + mc) * X]).astype(jnp.int32)
    n_rec, n_src = Z * X * 64, Y * C * 512
    grid = [(x, y) for x in range(X) for y in range(Y)]

    wave = {0: downgoing[:, 0]}
    wave |= {k % Z: send(wave[0], "z", Z, k) for k in (2, -2, 1, -1)}
    wave[3] = send(wave[2], "z", Z, 1)
    wave[5] = send(wave[6], "z", Z, -1)
    wave[4] = send(wave[2], "z", Z, 2)
    wave = [wave[k] for k in range(Z)]
    refl = reflectivity[:, 0]
    (refl,) = kernel_call(pair_kernel, [((C, 128, 256), BF)], [VMEM] * 2, "pair")(
        place, refl, send(refl, "c", C, 1)
    )
    refl = turn(refl, {(x, y): (y, x) for x, y in grid})
    refl = [refl] + [send(refl, "y", Y, k) for k in range(1, Y)]

    *pred, wave, refl = kernel_call(
        predict_kernel,
        [((128, 512), F32)] + [((144, 512), I16)] * 3 + [((Z, 64, 1024), BF), ((C, X, 128, 256), BF)],
        [VMEM] * 12,
        "predict",
        scratch=[pltpu.VMEM((X, 128, 1024), F32)],
    )(place, *refl, *wave)
    pred = [pred[0]] + [send(pred[k], "x", X, k) for k in range(1, X)]
    residual, coded = kernel_call(
        residual_kernel, [((2, 64, 512), F32), ((144, 512), I16)], [VMEM] * 6, "residual"
    )(place, *pred, upgoing[:, 0], recorded)
    coded = [coded] + [send(coded, "x", X, k) for k in range(1, X)]
    here, two, back, up, down, far, own, other = kernel_call(
        grads_kernel,
        [((128, 512), F32)] * 3
        + [((2, 144, 512), I16)] * 2
        + [((144, 512), I16)]
        + [((X, 128, 256), F32)] * 2,
        [VMEM] * 6,
        "grads",
        scratch=[pltpu.VMEM((X, 128, 1024), BF)] * 2 + [pltpu.VMEM((Z, 128, 512), F32)],
    )(place, refl, wave, *coded)
    up, down, far = send(up, "z", Z, 1), send(down, "z", Z, -1), send(far, "z", Z, 4)
    other = send(other, "c", C, 1)
    sums = kernel_call(core_sum_kernel, [((128, 256), F32)] * X, [VMEM] * 2, "core_sum")(
        place, own, other
    )
    up2, down2 = kernel_call(relay_kernel, [((144, 512), I16)] * 2, [VMEM] * 4 + [ANY], "relay")(
        place, two, back, up, down, sums[0]
    )
    up2, down2 = send(up2, "z", Z, 2), send(down2, "z", Z, -2)

    sums = [sums[0]] + [send(sums[k], "y", Y, k) for k in range(1, Y)]

    def last(*refs):
        last_kernel(n_rec ** (-0.5), n_src ** (-0.5), *refs)

    grad, base = kernel_call(
        refl_sum_kernel, [((128, 256), F32), ((128, 512), F32)], [VMEM] * 7, "refl_sum"
    )(place, *sums, here, up, down)
    grad = turn(grad, {(x, y): (y, x) for x, y in grid})
    grad_downgoing, grad_reflect = kernel_call(
        last, [((2, 64, 512), F32), ((2, 64, 256), F32)], [VMEM] * 5, "last"
    )(place, base, up2, down2, far, grad)
    return residual[:, None], grad_reflect[:, None], grad_downgoing[:, None]


def solution(mesh):
    fine = Mesh(mesh.devices.reshape(X, Z, Y, C), ("x", "z", "y", "c"))
    spec = P(None, None, ("x", "z"), ("y", "c"))
    return jax.shard_map(
        shards,
        mesh=fine,
        in_specs=(spec, spec, spec, P(("x", "z"), None)),
        out_specs=(spec, spec, spec),
        check_vma=False,
    )
```

```python
import jax
import jax.numpy as jnp
from jax import lax
from jax.experimental import pallas as pl
from jax.experimental.pallas import tpu as pltpu
from jax.sharding import Mesh, PartitionSpec as P

RBLK = 8
SBLK = 128
X, Z, Y, C = 4, 8, 4, 2
BF, F32, I16 = jnp.bfloat16, jnp.float32, jnp.int16
VMEM = pl.BlockSpec(memory_space=pltpu.VMEM)
ANY = pl.BlockSpec(memory_space=pl.ANY)
SMEM = pl.BlockSpec(memory_space=pltpu.SMEM)
PARAMS = pltpu.CompilerParams(vmem_limit_bytes=16 * 1024 * 1024)


def send(value, axis, size, step):
    return lax.ppermute(value, axis, [(i, (i + step) % size) for i in range(size)])


def turn(value, pairs):
    moves = [(x * Y + y, to[0] * Y + to[1]) for (x, y), to in pairs.items()]
    return lax.ppermute(value, ("x", "y"), moves)


def pair_kernel(place, mine, theirs, out):
    out[place[2]] = mine[...].reshape(128, 256)
    out[1 - place[2]] = theirs[...].reshape(128, 256)


def predict_kernel(place, *refs):
    rows, parts, (p0, p1, p2, p3, wave, refl, acc) = refs[:Y], refs[Y : Y + Z], refs[Y + Z :]
    mx, my, mz = place[0], place[1], place[3]
    for k, r in enumerate(rows):
        for c in range(C):
            refl[c, lax.rem(my - k + Y, Y)] = r[c]
    for zr, part in enumerate(parts):
        z = lax.rem(mz - zr + Z, Z)
        wave[z, :, 0:512] = part[0]
        wave[z, :, 512:1024] = part[1]
    total = jnp.zeros((512, 1024), F32)
    for c in range(C):
        w = wave[4 * c : 4 * c + 4].reshape(256, 1024)
        total += jnp.dot(refl[c].reshape(512, 256), w, preferred_element_type=F32)
    acc[...] = total.reshape(X, 128, 1024)
    for k, out in enumerate((p0, p1, p2, p3)):
        x = lax.rem(mx + k, X)
        a, b = acc[x, 0:64, :], acc[x, 64:128, :]
        real, imag = a[:, :512] - b[:, 512:], a[:, 512:] + b[:, :512]
        value = jnp.concatenate([real, imag], axis=0)
        if k:
            encode(value, out)
        else:
            out[...] = value


def residual_kernel(place, p0, p1, p2, p3, up, rec, res, coded):
    recs = rec[...]
    total = p0[...] + decode(p1) + decode(p2) + decode(p3)
    columns = []
    for k in range(X):
        hit = jnp.max(jnp.where(recs == place[4] + k, 1.0, 0.0), axis=1, keepdims=True)
        hit = jnp.broadcast_to(hit, (8, SBLK))
        columns.append(
            jnp.concatenate(
                [jnp.broadcast_to(hit[r : r + 1], (RBLK, SBLK)) for r in range(8)], axis=0
            )
        )
    mask = jnp.concatenate(columns, axis=1)
    parts = [mask * (total[64 * p : 64 * p + 64] - up[p].astype(F32)) for p in range(2)]
    res[0] = parts[0]
    res[1] = parts[1]
    encode(jnp.concatenate(parts, axis=0), coded)


def encode(value, out):
    rows = value.shape[0]
    most = jnp.max(jnp.abs(value), axis=0, keepdims=True)
    code = jnp.ceil(jnp.log2(jnp.maximum(most, 2.0**-100)) * 128.0 + 0.01)
    scaled = value * (jnp.exp2(code * (-1.0 / 128.0)) * 32767.0)
    scaled = jnp.clip(jnp.round(scaled), -32767.0, 32767.0)
    out[0:rows, :] = scaled.astype(jnp.int32).astype(jnp.int16)
    code = jnp.broadcast_to(code, (16, value.shape[1]))
    out[rows : rows + 16, :] = code.astype(jnp.int32).astype(jnp.int16)


def decode(coded):
    rows = coded.shape[0] - 16
    code = coded[rows : rows + 16, :].astype(jnp.int32).astype(F32)[0:1]
    scale = jnp.exp2(code * (1.0 / 128.0)) * (1.0 / 32767.0)
    return coded[0:rows, :].astype(jnp.int32).astype(F32) * scale


def scaled(value):
    most = jnp.max(jnp.abs(value), axis=0, keepdims=True)
    code = jnp.ceil(jnp.log2(jnp.maximum(most, 2.0**-100)) * 128.0 + 0.01)
    number = value * (jnp.exp2(code * (-1.0 / 128.0)) * 32767.0)
    return jnp.clip(jnp.round(number), -32767.0, 32767.0), code


def encode_pair(first, second, out):
    codes = []
    for i, value in enumerate((first, second)):
        number, code = scaled(value)
        out[128 * i : 128 * i + 128, :] = number.astype(jnp.int32).astype(jnp.int16)
        codes.append(jnp.broadcast_to(code, (8, value.shape[1])))
    out[256:272, :] = jnp.concatenate(codes, axis=0).astype(jnp.int32).astype(jnp.int16)


def decode_pair(coded, i):
    code = coded[256:272, :].astype(jnp.int32).astype(F32)[8 * i : 8 * i + 1]
    scale = jnp.exp2(code * (1.0 / 128.0)) * (1.0 / 32767.0)
    return coded[128 * i : 128 * i + 128, :].astype(jnp.int32).astype(F32) * scale


def grads_kernel(place, refl, wave, e0, e1, e2, e3, here, two, back, up, down, far, own, other, high, low, sums):
    mx, mc = place[0], place[2]
    for k, e in enumerate((e0, e1, e2, e3)):
        x = lax.rem(mx - k + X, X)
        value = decode(e)
        upper = value.astype(BF)
        lower = (value - upper.astype(F32)).astype(BF)
        for to, v in ((high, upper), (low, lower)):
            to[x, 0:64, 0:512] = v[0:64]
            to[x, 0:64, 512:1024] = v[64:128]
            to[x, 64:128, 0:512] = v[64:128]
            to[x, 64:128, 512:1024] = -v[0:64]
    h, l = high[...].reshape(512, 1024), low[...].reshape(512, 1024)
    for half in range(C):
        r = refl[half].reshape(512, 256)
        dims = (((0,), (0,)), ((), ()))
        g = lax.dot_general(r, h, dims, preferred_element_type=F32)
        g += lax.dot_general(r, l, dims, preferred_element_type=F32)
        for q in range(4):
            part = g[q * 64 : q * 64 + 64]
            part = jnp.concatenate([part[:, 0:512], part[:, 512:1024]], axis=0)
            sums[4 * half + q] = part
    def toward(step):
        return sums[lax.rem(place[3] + step + Z, Z)]

    here[...] = toward(0)
    two[...] = toward(2)
    back[...] = toward(-2)
    encode_pair(toward(1), toward(3), up)
    encode_pair(toward(-1), toward(-3), down)
    encode(toward(4), far)
    for to, half in ((own, mc), (other, 1 - mc)):
        w = wave[pl.ds(4 * half, 4)].reshape(256, 1024)
        dims = (((1,), (1,)), ((), ()))
        g = lax.dot_general(h, w, dims, preferred_element_type=F32)
        g += lax.dot_general(l, w, dims, preferred_element_type=F32)
        to[...] = g.reshape(X, 128, 256)


def core_sum_kernel(place, own, other, s0, s1, s2, s3):
    for k, out in enumerate((s0, s1, s2, s3)):
        x = lax.rem(place[1] + k, X)
        out[...] = own[x] + other[x]


def refl_sum_kernel(place, s0, s1, s2, s3, here, up, down, out, base):
    out[...] = (s0[...] + s1[...]) + (s2[...] + s3[...])
    base[...] = here[...] + decode_pair(up, 0) + decode_pair(down, 0)


def relay_kernel(place, two, back, up, down, after, out_up, out_down):
    encode(two[...] + decode_pair(up, 1), out_up)
    encode(back[...] + decode_pair(down, 1), out_down)


def last_kernel(scale, refl_scale, place, base, up2, down2, far, grad, out, refl_out):
    total = base[...] + decode(up2) + decode(down2) + decode(far)
    out[...] = (total * scale).reshape(2, 64, 512)
    refl_out[...] = (grad[...] * refl_scale).reshape(2, 64, 256)


def kernel_call(body, outs, ins, name, out_specs=None, aliases={}, scratch=()):
    return pl.pallas_call(
        body,
        out_shape=[jax.ShapeDtypeStruct(s, d) for s, d in outs],
        in_specs=[SMEM] + ins,
        out_specs=out_specs or [VMEM] * len(outs),
        input_output_aliases=aliases,
        scratch_shapes=scratch,
        compiler_params=PARAMS,
        name=name,
    )


def shards(reflectivity, downgoing, upgoing, recorded):
    mx, my, mc = lax.axis_index("x"), lax.axis_index("y"), lax.axis_index("c")
    place = jnp.stack([mx, my, mc, lax.axis_index("z"), (my * C + mc) * X]).astype(jnp.int32)
    n_rec, n_src = Z * X * 64, Y * C * 512
    grid = [(x, y) for x in range(X) for y in range(Y)]

    wave = {0: downgoing[:, 0]}
    wave |= {k % Z: send(wave[0], "z", Z, k) for k in (2, -2, 1, -1)}
    wave[3] = send(wave[2], "z", Z, 1)
    wave[5] = send(wave[6], "z", Z, -1)
    wave[4] = send(wave[2], "z", Z, 2)
    wave = [wave[k] for k in range(Z)]
    refl = reflectivity[:, 0]
    (refl,) = kernel_call(pair_kernel, [((C, 128, 256), BF)], [VMEM] * 2, "pair")(
        place, refl, send(refl, "c", C, 1)
    )
    refl = turn(refl, {(x, y): (y, x) for x, y in grid})
    refl = [refl] + [send(refl, "y", Y, k) for k in range(1, Y)]

    *pred, wave, refl = kernel_call(
        predict_kernel,
        [((128, 512), F32)] + [((144, 512), I16)] * 3 + [((Z, 64, 1024), BF), ((C, X, 128, 256), BF)],
        [VMEM] * 12,
        "predict",
        scratch=[pltpu.VMEM((X, 128, 1024), F32)],
    )(place, *refl, *wave)
    pred = [pred[0]] + [send(pred[k], "x", X, k) for k in range(1, X)]
    residual, coded = kernel_call(
        residual_kernel, [((2, 64, 512), F32), ((144, 512), I16)], [VMEM] * 6, "residual"
    )(place, *pred, upgoing[:, 0], recorded)
    coded = [coded] + [send(coded, "x", X, k) for k in range(1, X)]
    here, two, back, up, down, far, own, other = kernel_call(
        grads_kernel,
        [((128, 512), F32)] * 3
        + [((272, 512), I16)] * 2
        + [((144, 512), I16)]
        + [((X, 128, 256), F32)] * 2,
        [VMEM] * 6,
        "grads",
        scratch=[pltpu.VMEM((X, 128, 1024), BF)] * 2 + [pltpu.VMEM((Z, 128, 512), F32)],
    )(place, refl, wave, *coded)
    up, down, far = send(up, "z", Z, 1), send(down, "z", Z, -1), send(far, "z", Z, 4)
    other = send(other, "c", C, 1)
    sums = kernel_call(core_sum_kernel, [((128, 256), F32)] * X, [VMEM] * 2, "core_sum")(
        place, own, other
    )
    up2, down2 = kernel_call(relay_kernel, [((144, 512), I16)] * 2, [VMEM] * 4 + [ANY], "relay")(
        place, two, back, up, down, sums[0]
    )
    up2, down2 = send(up2, "z", Z, 2), send(down2, "z", Z, -2)

    sums = [sums[0]] + [send(sums[k], "y", Y, k) for k in range(1, Y)]

    def last(*refs):
        last_kernel(n_rec ** (-0.5), n_src ** (-0.5), *refs)

    grad, base = kernel_call(
        refl_sum_kernel, [((128, 256), F32), ((128, 512), F32)], [VMEM] * 7, "refl_sum"
    )(place, *sums, here, up, down)
    grad = turn(grad, {(x, y): (y, x) for x, y in grid})
    grad_downgoing, grad_reflect = kernel_call(
        last, [((2, 64, 512), F32), ((2, 64, 256), F32)], [VMEM] * 5, "last"
    )(place, base, up2, down2, far, grad)
    return residual[:, None], grad_reflect[:, None], grad_downgoing[:, None]


def solution(mesh):
    fine = Mesh(mesh.devices.reshape(X, Z, Y, C), ("x", "z", "y", "c"))
    spec = P(None, None, ("x", "z"), ("y", "c"))
    return jax.shard_map(
        shards,
        mesh=fine,
        in_specs=(spec, spec, spec, P(("x", "z"), None)),
        out_specs=(spec, spec, spec),
        check_vma=False,
    )
```
